32 devices in a mesh: dp: 8 (over z, y), tensor: 4 (over x, core).
Axes of the slice: x: 2, y: 2, z: 4, core: 2. Of those that a mesh axis runs over, the one named last changes fastest.
Arguments:
- inputs: bfloat16 [2048, 6144], P('dp', 'tensor'), may hold values from -250 to 250
- upstream: bfloat16 [2048, 1024], P('dp', 'tensor'), may hold values from -6 to 6
- proj_weight: bfloat16 [6144, 1024], P(None, 'tensor'), may hold values from -0.078125 to 0.078125
- proj_bias: float32 [1024], P('tensor'), may hold values from -4 to 4
- norm_gain: float32 [6144], replicated, may hold values from 0.1 to 1.9
- home_rows: int32 [2048], P('dp'), may hold values from 0 to 2047, as said below
Outputs:
- home_grad: bfloat16 [2048, 6144], P('dp', 'tensor')
The draws below stay inside these ranges and needn't reach their ends.
Inputs may be any that keep to these rules, and one draw needn't show every extreme that they name: `home_rows`: A permutation of 0 to 2047. The balanced row at position i * 256 + k goes to a home row j * 256 + s (0 <= s < 256); of the 256 rows of one dp index, at most 64 have the same owner j, and in every draw some do.
All inputs are finite; a program needn't handle non-finite values.
Results may differ from the reference program's by a relative error of at most 0.018.
Values may be sent and summed in bfloat16 or wider, within the bound.
A program may use at most 64 MiB of HBM per device.

```python
import math
import jax
import jax.numpy as jnp
from jax import lax

D = 6144
HEAD_DIM = 256
ROW_DEV = 256
CAPACITY = 64
HEADS = 4
COLS = 1024
ROWS = 2048
N_DP = 8


def draw_inputs(key, part):
    first, second, third = jax.random.split(key, 3)
    row_scale = jnp.exp(jax.random.uniform(first, (ROWS, 1), jnp.float32, math.log(0.5), math.log(5.0)))
    col_scale = jnp.exp(jax.random.uniform(second, (1, D), jnp.float32, math.log(0.5), math.log(5.0)))
    return (jax.random.normal(third, (ROWS, D), jnp.float32) * row_scale * col_scale).astype(jnp.bfloat16)


def home_block(key):
    first, second, third = jax.random.split(key, 3)
    identifiers = jnp.arange(N_DP * CAPACITY, dtype=jnp.int32)
    shuffled = jax.random.permutation(first, identifiers)
    placed_at = jnp.zeros((N_DP * CAPACITY,), jnp.int32).at[shuffled].set(identifiers)
    labels = identifiers // CAPACITY
    forced = shuffled[0] // CAPACITY
    ranking = jnp.where(labels == forced, identifiers - N_DP * CAPACITY, placed_at)
    ordering = jnp.argsort(ranking)
    chosen = labels[ordering[:ROW_DEV]]
    offsets = jax.random.permutation(second, chosen)
    within_owner = jax.vmap(lambda subkey: jax.random.permutation(subkey, jnp.arange(ROW_DEV, dtype=jnp.int32)))(jax.random.split(third, N_DP))
    sources = jnp.arange(N_DP, dtype=jnp.int32)[:, None]
    owner_of = (sources + offsets[None, :]) % N_DP
    home_slot = within_owner[owner_of, jnp.arange(ROW_DEV, dtype=jnp.int32)[None, :]]
    return owner_of * ROW_DEV + home_slot


def draw_home_rows(key, part):
    return home_block(key).reshape(-1).astype(jnp.int32)


def with_spikes(drawn, stream_key, source, target, parts, factor):
    owner, partner = [(jnp.arange(drawn.shape[position]) // (drawn.shape[position] // parts)).reshape([-1 if axis == position else 1 for axis in range(drawn.ndim)]) for position in (source, target)]
    chosen = jax.random.permutation(stream_key, parts)[partner]
    strong = (owner == chosen) | (owner == (partner + parts // 2) % parts)
    return jnp.where(strong, factor * drawn, drawn)


def block_levels(own_key, shape, cuts, least, high):
    loudness = 1.0
    for dim, parts in cuts:
        heights = jax.random.uniform(jax.random.fold_in(jax.random.fold_in(own_key, 6), dim), (parts,), jnp.float32, least / len(cuts), high / len(cuts))
        loudness = loudness * jnp.repeat(jnp.exp(heights), shape[dim] // parts).reshape((-1,) + (1,) * (len(shape) - 1 - dim))
    return loudness


def gaussian(own_key, shape, width, bound, shards=(), kind=jnp.bfloat16):
    values = width * jax.random.normal(own_key, shape, jnp.float32)
    if shards:
        values = values * block_levels(own_key, shape, shards, -0.22, 0.18)
    return jnp.clip(values, -bound, bound).astype(kind)


def heavy_noise(rng, extent, width, limit, cuts, heavy, kind=jnp.bfloat16):
    values = width * jax.random.normal(rng, extent, jnp.float32)
    if cuts:
        values = values * block_levels(rng, extent, cuts, -0.22, 0.18)
    return jnp.clip(with_spikes(values, jax.random.fold_in(rng, 3), *heavy), -limit, limit).astype(kind)


def setup_inputs(seed: int = 0) -> dict:
    key_of = jax.random.split(jax.random.key(seed), 7)
    inputs = draw_inputs(jax.random.fold_in(key_of[6], 71), 0)
    upstream = heavy_noise(key_of[1], (ROWS, COLS), 1.0, 6.0, ((0, 8), (1, 4)), (1, 0, 8, 2.0))
    proj_weight = gaussian(key_of[2], (D, COLS), D ** -0.5, 0.078125, ((1, 4),))
    proj_bias = gaussian(key_of[3], (COLS,), 1.0, 4.0, ((0, 4),), jnp.float32)
    norm_gain = jnp.clip(1.0 + 0.18 * jax.random.normal(key_of[4], (D,), jnp.float32), 0.1, 1.9)
    home_rows = draw_home_rows(jax.random.fold_in(key_of[6], 71), 0)
    return dict(inputs=inputs, upstream=upstream, proj_weight=proj_weight, proj_bias=proj_bias, norm_gain=norm_gain, home_rows=home_rows)


epsilon = 1e-05

def contract_cols(left, right):
    return lax.dot_general(left.astype(jnp.float32), right.astype(jnp.float32), (((1,), (1,)), ((), ())), preferred_element_type=jnp.float32)

def reference(inputs, upstream, proj_weight, proj_bias, norm_gain, home_rows):
    widened = inputs.astype(jnp.float32)
    row_mean = lax.optimization_barrier(jnp.mean(widened, axis=1, keepdims=True))
    centred = widened - row_mean
    inv_std = lax.rsqrt(lax.optimization_barrier(jnp.mean(centred * centred, axis=1, keepdims=True)) + epsilon)
    unit_rows = centred * inv_std
    normed = (unit_rows * norm_gain[None, :]).astype(jnp.bfloat16)
    preact = jnp.dot(normed, proj_weight, preferred_element_type=jnp.float32) + proj_bias[None, :]
    gate_value = jax.nn.sigmoid(preact)
    pre_grad = (upstream.astype(jnp.float32) * gate_value * (1.0 + preact * (1.0 - gate_value))).astype(jnp.bfloat16)

    def add_head(head, total):
        start = (head * HEAD_DIM).astype(jnp.int32)
        part_grad = lax.dynamic_slice_in_dim(pre_grad, start, HEAD_DIM, 1)
        part_weight = lax.dynamic_slice_in_dim(proj_weight, start, HEAD_DIM, 1)
        term = contract_cols(part_grad, part_weight).astype(jnp.bfloat16)
        return total + lax.optimization_barrier(term).astype(jnp.float32)
    summed = lax.fori_loop(0, HEADS, add_head, jnp.zeros((ROWS, D), jnp.float32))
    scaled = summed * norm_gain[None, :]
    input_grad = (inv_std * (scaled - lax.optimization_barrier(jnp.mean(scaled, axis=1, keepdims=True)) - unit_rows * lax.optimization_barrier(jnp.mean(scaled * unit_rows, axis=1, keepdims=True)))).astype(jnp.bfloat16)
    return jnp.zeros((ROWS, D), jnp.bfloat16).at[home_rows.astype(jnp.int32)].set(input_grad)
```

```python
import functools
import math

import jax
import jax.numpy as jnp
from jax import lax
from jax.experimental import pallas as pl
from jax.experimental.pallas import tpu as pltpu
from jax.sharding import PartitionSpec as P

epsilon = 1e-05
MESH = pl.DeviceIdType.MESH
f32, bf16 = jnp.float32, jnp.bfloat16
LANES = 128


def rows_by_cols(left, right):
    return lax.dot_general(
        left, right, (((1,), (1,)), ((), ())), preferred_element_type=f32
    )


def kernel(
    n_dp, n_t, cap,
    x_ref, up_ref, w_ref, bias_ref, gain_ref, hr_col_ref, hr_row_ref,
    out_ref,
    weights, packed, arrived, slots_out, slots_in, home, centred,
    part_out, part_in, stat_out, stat_in, grads, sums,
    w_send, w_recv, row_send, row_recv, slot_send, slot_recv,
    part_send, part_recv, stat_send, stat_recv, grad_send, grad_recv, sum_send, sum_recv,
    local_sem,
):
    me = lax.axis_index("dp")
    t = lax.axis_index("tensor")
    rows, cols = x_ref.shape
    head = up_ref.shape[1]
    width = cols + head
    depth = n_t * cols
    per = LANES // cap

    def sibling(u):
        return u + 1 - 2 * lax.rem(u, 2)

    peers = []
    for k in range(1, n_t // 2):
        u = lax.rem(t + 2 * k, n_t)
        peers += [u, sibling(u)]
    peers.append(sibling(t))
    dests = [lax.rem(me + d, n_dp) for d in range(1, n_dp)]
    sources = [lax.rem(me + n_dp - d, n_dp) for d in range(1, n_dp)]

    barrier = pltpu.get_barrier_semaphore()
    for u in peers:
        pl.semaphore_signal(barrier, inc=1, device_id={"tensor": u}, device_id_type=MESH)
    for j in dests:
        pl.semaphore_signal(barrier, inc=1, device_id={"dp": j}, device_id_type=MESH)

    own_w = pltpu.make_async_copy(
        w_ref.at[pl.ds(pl.multiple_of(t * cols, LANES), cols)], weights.at[t], local_sem.at[0]
    )
    own_w.start()

    hr_col, hr_row = hr_col_ref[...], hr_row_ref[...]
    owner_col, owner_row = hr_col // rows, hr_row // rows
    slot_col = hr_col - owner_col * rows
    down = lax.broadcasted_iota(jnp.int32, (rows, rows), 0)
    across = lax.broadcasted_iota(jnp.int32, (rows, rows), 1)
    same = owner_col == owner_row
    rank_row = jnp.sum(jnp.where(same & (down < across), 1.0, 0.0), axis=0, keepdims=True).astype(jnp.int32)
    rank_col = jnp.sum(jnp.where(same & (across < down), 1.0, 0.0), axis=1, keepdims=True).astype(jnp.int32)
    target_row = owner_row * cap + rank_row
    total_slots = n_dp * cap
    placing = jnp.where(
        lax.broadcasted_iota(jnp.int32, (total_slots, rows), 0) == target_row, 1.0, 0.0
    ).astype(bf16)
    chunk = math.gcd(cols, 256)
    for c in range(0, cols, chunk):
        packed[:, c : c + chunk] = jnp.dot(
            placing, x_ref[:, c : c + chunk], preferred_element_type=f32
        ).astype(bf16)
    packed[:, cols:] = jnp.dot(placing, up_ref[...], preferred_element_type=f32).astype(bf16)
    lane = lax.broadcasted_iota(jnp.int32, (rows, LANES), 1)
    my_lane = lax.rem(me, per) * cap
    for j in range(n_dp):
        hit = (owner_col == j) & (rank_col + my_lane == lane)
        line = jnp.sum(jnp.where(hit, slot_col.astype(f32) + 1.0, 0.0), axis=0, keepdims=True)
        slots_out[j] = jnp.broadcast_to(line, (8, LANES)).astype(jnp.int32)

    def w_copy(u, src_slot):
        return pltpu.make_async_remote_copy(
            src_ref=w_ref.at[pl.ds(pl.multiple_of(u * cols, LANES), cols)],
            dst_ref=weights.at[src_slot],
            send_sem=w_send.at[u], recv_sem=w_recv.at[src_slot],
            device_id={"tensor": u}, device_id_type=MESH,
        )

    def row_copy(j, src_slot):
        return pltpu.make_async_remote_copy(
            src_ref=packed.at[pl.ds(pl.multiple_of(j * cap, 16), cap)],
            dst_ref=arrived.at[pl.ds(pl.multiple_of(src_slot * cap, 16), cap)],
            send_sem=row_send.at[j], recv_sem=row_recv.at[src_slot],
            device_id={"dp": j}, device_id_type=MESH,
        )

    def slot_copy(j, src_slot):
        return pltpu.make_async_remote_copy(
            src_ref=slots_out.at[j], dst_ref=slots_in.at[src_slot],
            send_sem=slot_send.at[j], recv_sem=slot_recv.at[src_slot],
            device_id={"dp": j}, device_id_type=MESH,
        )

    def tensor_copy(src, dst, send, recv, u, src_slot):
        return pltpu.make_async_remote_copy(
            src_ref=src, dst_ref=dst.at[src_slot],
            send_sem=send.at[u], recv_sem=recv.at[src_slot],
            device_id={"tensor": u}, device_id_type=MESH,
        )

    pl.semaphore_wait(barrier, len(peers) + len(dests))
    for u in peers:
        w_copy(u, t).start()
    for j in dests:
        slot_copy(j, me).start()
        row_copy(j, me).start()
    own_rows = pltpu.make_async_copy(
        packed.at[pl.ds(pl.multiple_of(me * cap, 16), cap)],
        arrived.at[pl.ds(pl.multiple_of(me * cap, 16), cap)],
        local_sem.at[1],
    )
    own_rows.start()
    slots_in[me] = slots_out[me]

    gain = gain_ref[pl.ds(t, 1), :]
    gain_hi = gain.astype(bf16)
    gain_rest = gain - gain_hi.astype(f32)
    gain_mid = gain_rest.astype(bf16)
    gain_lo = (gain_rest - gain_mid.astype(f32)).astype(bf16)
    which = lax.broadcasted_iota(jnp.int32, (16, cols), 0)
    gain_parts = jnp.where(
        which == 0, gain_hi.astype(f32),
        jnp.where(which == 1, gain_mid.astype(f32), jnp.where(which == 2, gain_lo.astype(f32), 0.0)),
    ).astype(bf16)

    def weighted_sum(u):
        stat_out[u] = jnp.zeros(stat_out.shape[1:], f32)
        line = jnp.sum(jnp.dot(gain_parts, weights[u], preferred_element_type=f32), axis=0, keepdims=True)
        stat_out[u, 2:3, :] = line

    own_w.wait()
    weighted_sum(t)
    for u in reversed(peers):
        w_copy(u, u).wait_recv()
        weighted_sum(u)

    for i in sources:
        slot_copy(i, i).wait_recv()
    lines = []
    for g in range(n_dp // per):
        line = slots_in[g * per, 0:1, :]
        for k in range(1, per):
            line = line + slots_in[g * per + k, 0:1, :]
        lines.append(line)
    slot_line = jnp.concatenate(lines, axis=1) - 1
    landing = jnp.where(
        lax.broadcasted_iota(jnp.int32, (rows, total_slots), 0) == slot_line, 1.0, 0.0
    ).astype(bf16)
    own_rows.wait()
    for i in sources:
        row_copy(i, i).wait_recv()
    running = jnp.zeros((rows, LANES), f32)
    for c in range(0, cols, chunk):
        piece = jnp.dot(landing, arrived[:, c : c + chunk], preferred_element_type=f32)
        home[:, c : c + chunk] = piece.astype(bf16)
        for q in range(0, chunk, LANES):
            running = running + piece[:, q : q + LANES]
    home[:, cols:] = jnp.dot(landing, arrived[:, cols:], preferred_element_type=f32).astype(bf16)
    mean_here = jnp.sum(running, axis=1, keepdims=True) / cols
    running = jnp.zeros((rows, LANES), f32)
    for c in range(0, cols, chunk):
        piece = home[:, c : c + chunk].astype(f32) - mean_here
        centred[:, c : c + chunk] = (piece * gain[:, c : c + chunk]).astype(bf16)
        square = piece * piece
        for q in range(0, chunk, LANES):
            running = running + square[:, q : q + LANES]
    moment_here = jnp.sum(running, axis=1, keepdims=True)

    eye = down == across

    def to_row(column):
        return jnp.sum(jnp.where(eye, column, 0.0), axis=0, keepdims=True)

    def to_col(line):
        return jnp.sum(jnp.where(eye, line, 0.0), axis=1, keepdims=True)

    mean_line, moment_line = to_row(mean_here), to_row(moment_here)
    for u in peers + [t]:
        stat_out[u, 0:1, :] = mean_line
        stat_out[u, 1:2, :] = moment_line
    for u in peers:
        tensor_copy(stat_out.at[u], stat_in, stat_send, stat_recv, u, t).start()
    for u in peers:
        part_out[u] = jnp.dot(centred[...], weights[u], preferred_element_type=f32).astype(bf16)
        tensor_copy(part_out.at[u], part_in, part_send, part_recv, u, t).start()
    total = jnp.dot(centred[...], weights[t], preferred_element_type=f32)

    stat_in[t] = stat_out[t]
    for u in peers:
        tensor_copy(stat_out.at[u], stat_in, stat_send, stat_recv, u, u).wait_recv()
    mean_all = stat_in[0, 0:1, :]
    moment_all = stat_in[0, 1:2, :]
    weighted = stat_in[0, 2:3, :]
    for u in range(1, n_t):
        mean_all = mean_all + stat_in[u, 0:1, :]
        moment_all = moment_all + stat_in[u, 1:2, :]
        weighted = weighted + stat_in[u, 2:3, :]
    mean_all = mean_all / n_t
    for u in range(n_t):
        away = stat_in[u, 0:1, :] - mean_all
        moment_all = moment_all + cols * away * away
        total = total + to_col(away) * stat_in[u, 2:3, :]
    scale = to_col(lax.rsqrt(moment_all / depth + epsilon))
    mean_col = to_col(mean_all)
    for u in peers:
        tensor_copy(part_out.at[u], part_in, part_send, part_recv, u, u).wait_recv()
        total = total + part_in[u].astype(f32)
    product = scale * total
    preact = product + bias_ref[...]
    gate = 1.0 / (1.0 + jnp.exp(-preact))
    grad = (home[:, cols:].astype(f32) * gate * (1.0 + preact * (1.0 - gate))).astype(bf16)
    grads[t] = grad
    for u in peers:
        tensor_copy(grads.at[t], grads, grad_send, grad_recv, u, t).start()
    wide = grad.astype(f32)
    sums[t] = jnp.zeros(sums.shape[1:], f32)
    sums[t, 0:1, :] = to_row(jnp.sum(wide * weighted, axis=1, keepdims=True))
    sums[t, 1:2, :] = to_row(jnp.sum(wide * product, axis=1, keepdims=True))
    for u in peers:
        tensor_copy(sums.at[t], sums, sum_send, sum_recv, u, t).start()
    for u in peers:
        tensor_copy(sums.at[t], sums, sum_send, sum_recv, u, u).wait_recv()
    both = sums[0]
    for u in range(1, n_t):
        both = both + sums[u]
    mean_grad = to_col(both[0:1, :]) / depth
    mean_unit = to_col(both[1:2, :]) / depth * scale
    for u in peers:
        tensor_copy(grads.at[t], grads, grad_send, grad_recv, u, u).wait_recv()
    for c in range(0, cols, chunk):
        piece = rows_by_cols(grads[0], weights[0, c : c + chunk, :])
        for u in range(1, n_t):
            piece = piece + rows_by_cols(grads[u], weights[u, c : c + chunk, :])
        piece = piece * gain[:, c : c + chunk]
        away = home[:, c : c + chunk].astype(f32) - mean_col
        out_ref[:, c : c + chunk] = (scale * (piece - mean_grad - away * mean_unit)).astype(bf16)

    for u in peers:
        w_copy(u, t).wait_send()
        tensor_copy(stat_out.at[u], stat_in, stat_send, stat_recv, u, t).wait_send()
        tensor_copy(part_out.at[u], part_in, part_send, part_recv, u, t).wait_send()
        tensor_copy(grads.at[t], grads, grad_send, grad_recv, u, t).wait_send()
        tensor_copy(sums.at[t], sums, sum_send, sum_recv, u, t).wait_send()
    for j in dests:
        slot_copy(j, me).wait_send()
        row_copy(j, me).wait_send()


def per_device(inputs, upstream, proj_weight, proj_bias, norm_gain, home_rows):
    n_dp, n_t = lax.axis_size("dp"), lax.axis_size("tensor")
    rows, cols = inputs.shape
    head = upstream.shape[1]
    cap = max(2, 2 * rows // n_dp)
    width = cols + head
    line = max(rows, head)
    dma = pltpu.SemaphoreType.DMA
    in_vmem = pl.BlockSpec(memory_space=pltpu.VMEM)
    return pl.pallas_call(
        functools.partial(kernel, n_dp, n_t, cap),
        out_shape=jax.ShapeDtypeStruct((rows, cols), bf16),
        in_specs=[in_vmem, in_vmem, pl.BlockSpec(memory_space=pl.ANY)] + [in_vmem] * 4,
        out_specs=in_vmem,
        scratch_shapes=[
            pltpu.VMEM((n_t, cols, head), bf16),
            pltpu.VMEM((n_dp * cap, width), bf16),
            pltpu.VMEM((n_dp * cap, width), bf16),
            pltpu.VMEM((n_dp, 8, LANES), jnp.int32),
            pltpu.VMEM((n_dp, 8, LANES), jnp.int32),
            pltpu.VMEM((rows, width), bf16),
            pltpu.VMEM((rows, cols), bf16),
            pltpu.VMEM((n_t, rows, head), bf16),
            pltpu.VMEM((n_t, rows, head), bf16),
            pltpu.VMEM((n_t, 8, line), f32),
            pltpu.VMEM((n_t, 8, line), f32),
            pltpu.VMEM((n_t, rows, head), bf16),
            pltpu.VMEM((n_t, 8, line), f32),
        ]
        + [dma((n_t,))] * 2
        + [dma((n_dp,))] * 4
        + [dma((n_t,))] * 8
        + [dma((2,))],
        compiler_params=pltpu.CompilerParams(
            collective_id=0, has_side_effects=True, vmem_limit_bytes=48 * 1024 * 1024
        ),
        cost_estimate=pl.CostEstimate(
            flops=8 * rows * cols * head * n_t, bytes_accessed=2 * n_t * cols * head, transcendentals=rows * head
        ),
    )(
        inputs,
        upstream,
        proj_weight,
        proj_bias.reshape(1, head),
        norm_gain.reshape(n_t, cols),
        home_rows.reshape(rows, 1),
        home_rows.reshape(1, rows),
    )


def solution(mesh):
    return jax.shard_map(
        per_device,
        mesh=mesh,
        in_specs=(
            P("dp", "tensor"),
            P("dp", "tensor"),
            P(None, "tensor"),
            P("tensor"),
            P(),
            P("dp"),
        ),
        out_specs=P("dp", "tensor"),
        check_vma=False,
    )
```

```python
import functools
import math

import jax
import jax.numpy as jnp
from jax import lax
from jax.experimental import pallas as pl
from jax.experimental.pallas import tpu as pltpu
from jax.sharding import PartitionSpec as P

epsilon = 1e-05
MESH = pl.DeviceIdType.MESH
f32, bf16 = jnp.float32, jnp.bfloat16
LANES = 128


def rows_by_cols(left, right):
    return lax.dot_general(
        left, right, (((1,), (1,)), ((), ())), preferred_element_type=f32
    )


def kernel(
    n_dp, n_t, cap,
    x_hbm, up_hbm, w_ref, bias_hbm, gain_hbm, hr_hbm,
    out_ref,
    x_ref, up_ref, bias_ref, gain_ref, hr_ref,
    weights, packed, arrived, slots_out, slots_in, home, centred,
    part_out, part_in, stat_out, stat_in, grads, sums,
    w_send, w_recv, row_send, row_recv, slot_send, slot_recv,
    part_send, part_recv, stat_send, stat_recv, grad_send, grad_recv, sum_send, sum_recv,
    local_sem,
):
    me = lax.axis_index("dp")
    t = lax.axis_index("tensor")
    rows, cols = x_ref.shape
    head = up_ref.shape[1]
    width = cols + head
    depth = n_t * cols
    per = LANES // cap

    def sibling(u):
        return u + 1 - 2 * lax.rem(u, 2)

    peers = []
    for k in range(1, n_t // 2):
        u = lax.rem(t + 2 * k, n_t)
        peers += [u, sibling(u)]
    peers.append(sibling(t))
    dests = [lax.rem(me + d, n_dp) for d in range(1, n_dp)]
    sources = [lax.rem(me + n_dp - d, n_dp) for d in range(1, n_dp)]

    barrier = pltpu.get_barrier_semaphore()
    for u in peers:
        pl.semaphore_signal(barrier, inc=1, device_id={"tensor": u}, device_id_type=MESH)
    for j in dests:
        pl.semaphore_signal(barrier, inc=1, device_id={"dp": j}, device_id_type=MESH)

    own_w = pltpu.make_async_copy(
        w_ref.at[pl.ds(pl.multiple_of(t * cols, LANES), cols)], weights.at[t], local_sem.at[0]
    )
    fetches = [
        pltpu.make_async_copy(src, dst, local_sem.at[2 + k])
        for k, (src, dst) in enumerate(
            [
                (hr_hbm, hr_ref),
                (x_hbm, x_ref),
                (up_hbm, up_ref),
                (gain_hbm.at[:, pl.ds(pl.multiple_of(t * cols, LANES), cols)], gain_ref),
                (bias_hbm, bias_ref),
            ]
        )
    ]
    for fetch in fetches:
        fetch.start()
    own_w.start()

    fetches[0].wait()
    hr_row = hr_ref[...]
    down = lax.broadcasted_iota(jnp.int32, (rows, rows), 0)
    across = lax.broadcasted_iota(jnp.int32, (rows, rows), 1)
    eye = down == across
    hr_col = jnp.sum(jnp.where(eye, hr_row.astype(f32), 0.0), axis=1, keepdims=True).astype(jnp.int32)
    owner_col, owner_row = hr_col // rows, hr_row // rows
    slot_col = hr_col - owner_col * rows
    same = owner_col == owner_row
    rank_row = jnp.sum(jnp.where(same & (down < across), 1.0, 0.0), axis=0, keepdims=True).astype(jnp.int32)
    rank_col = jnp.sum(jnp.where(same & (across < down), 1.0, 0.0), axis=1, keepdims=True).astype(jnp.int32)
    target_row = owner_row * cap + rank_row
    total_slots = n_dp * cap
    placing = jnp.where(
        lax.broadcasted_iota(jnp.int32, (total_slots, rows), 0) == target_row, 1.0, 0.0
    ).astype(bf16)
    chunk = math.gcd(cols, 256)
    fetches[1].wait()
    fetches[2].wait()
    for c in range(0, cols, chunk):
        packed[:, c : c + chunk] = jnp.dot(
            placing, x_ref[:, c : c + chunk], preferred_element_type=f32
        ).astype(bf16)
    packed[:, cols:] = jnp.dot(placing, up_ref[...], preferred_element_type=f32).astype(bf16)
    lane = lax.broadcasted_iota(jnp.int32, (rows, LANES), 1)
    my_lane = lax.rem(me, per) * cap
    for j in range(n_dp):
        hit = (owner_col == j) & (rank_col + my_lane == lane)
        line = jnp.sum(jnp.where(hit, slot_col.astype(f32) + 1.0, 0.0), axis=0, keepdims=True)
        slots_out[j] = jnp.broadcast_to(line, (8, LANES)).astype(jnp.int32)

    def w_copy(u, src_slot):
        return pltpu.make_async_remote_copy(
            src_ref=w_ref.at[pl.ds(pl.multiple_of(u * cols, LANES), cols)],
            dst_ref=weights.at[src_slot],
            send_sem=w_send.at[u], recv_sem=w_recv.at[src_slot],
            device_id={"tensor": u}, device_id_type=MESH,
        )

    def row_copy(j, src_slot):
        return pltpu.make_async_remote_copy(
            src_ref=packed.at[pl.ds(pl.multiple_of(j * cap, 16), cap)],
            dst_ref=arrived.at[pl.ds(pl.multiple_of(src_slot * cap, 16), cap)],
            send_sem=row_send.at[j], recv_sem=row_recv.at[src_slot],
            device_id={"dp": j}, device_id_type=MESH,
        )

    def slot_copy(j, src_slot):
        return pltpu.make_async_remote_copy(
            src_ref=slots_out.at[j], dst_ref=slots_in.at[src_slot],
            send_sem=slot_send.at[j], recv_sem=slot_recv.at[src_slot],
            device_id={"dp": j}, device_id_type=MESH,
        )

    def tensor_copy(src, dst, send, recv, u, src_slot):
        return pltpu.make_async_remote_copy(
            src_ref=src, dst_ref=dst.at[src_slot],
            send_sem=send.at[u], recv_sem=recv.at[src_slot],
            device_id={"tensor": u}, device_id_type=MESH,
        )

    pl.semaphore_wait(barrier, len(peers) + len(dests))
    for u in peers:
        w_copy(u, t).start()
    for j in dests:
        slot_copy(j, me).start()
        row_copy(j, me).start()
    own_rows = pltpu.make_async_copy(
        packed.at[pl.ds(pl.multiple_of(me * cap, 16), cap)],
        arrived.at[pl.ds(pl.multiple_of(me * cap, 16), cap)],
        local_sem.at[1],
    )
    own_rows.start()
    slots_in[me] = slots_out[me]

    fetches[3].wait()
    fetches[4].wait()
    gain = gain_ref[...]
    gain_hi = gain.astype(bf16)
    gain_rest = gain - gain_hi.astype(f32)
    gain_mid = gain_rest.astype(bf16)
    gain_lo = (gain_rest - gain_mid.astype(f32)).astype(bf16)
    which = lax.broadcasted_iota(jnp.int32, (16, cols), 0)
    gain_parts = jnp.where(
        which == 0, gain_hi.astype(f32),
        jnp.where(which == 1, gain_mid.astype(f32), jnp.where(which == 2, gain_lo.astype(f32), 0.0)),
    ).astype(bf16)

    def weighted_sum(u):
        stat_out[u] = jnp.zeros(stat_out.shape[1:], f32)
        line = jnp.sum(jnp.dot(gain_parts, weights[u], preferred_element_type=f32), axis=0, keepdims=True)
        stat_out[u, 2:3, :] = line

    own_w.wait()
    weighted_sum(t)
    for u in reversed(peers):
        w_copy(u, u).wait_recv()
        weighted_sum(u)

    for i in sources:
        slot_copy(i, i).wait_recv()
    lines = []
    for g in range(n_dp // per):
        line = slots_in[g * per, 0:1, :]
        for k in range(1, per):
            line = line + slots_in[g * per + k, 0:1, :]
        lines.append(line)
    slot_line = jnp.concatenate(lines, axis=1) - 1
    landing = jnp.where(
        lax.broadcasted_iota(jnp.int32, (rows, total_slots), 0) == slot_line, 1.0, 0.0
    ).astype(bf16)
    own_rows.wait()
    for i in sources:
        row_copy(i, i).wait_recv()
    running = jnp.zeros((rows, LANES), f32)
    for c in range(0, cols, chunk):
        piece = jnp.dot(landing, arrived[:, c : c + chunk], preferred_element_type=f32)
        home[:, c : c + chunk] = piece.astype(bf16)
        for q in range(0, chunk, LANES):
            running = running + piece[:, q : q + LANES]
    home[:, cols:] = jnp.dot(landing, arrived[:, cols:], preferred_element_type=f32).astype(bf16)
    mean_here = jnp.sum(running, axis=1, keepdims=True) / cols
    running = jnp.zeros((rows, LANES), f32)
    for c in range(0, cols, chunk):
        piece = home[:, c : c + chunk].astype(f32) - mean_here
        centred[:, c : c + chunk] = (piece * gain[:, c : c + chunk]).astype(bf16)
        square = piece * piece
        for q in range(0, chunk, LANES):
            running = running + square[:, q : q + LANES]
    moment_here = jnp.sum(running, axis=1, keepdims=True)

    def to_row(column):
        return jnp.sum(jnp.where(eye, column, 0.0), axis=0, keepdims=True)

    def to_col(line):
        return jnp.sum(jnp.where(eye, line, 0.0), axis=1, keepdims=True)

    mean_line, moment_line = to_row(mean_here), to_row(moment_here)
    for u in peers + [t]:
        stat_out[u, 0:1, :] = mean_line
        stat_out[u, 1:2, :] = moment_line
    for u in peers:
        tensor_copy(stat_out.at[u], stat_in, stat_send, stat_recv, u, t).start()
    for u in peers:
        part_out[u] = jnp.dot(centred[...], weights[u], preferred_element_type=f32).astype(bf16)
        tensor_copy(part_out.at[u], part_in, part_send, part_recv, u, t).start()
    total = jnp.dot(centred[...], weights[t], preferred_element_type=f32)

    stat_in[t] = stat_out[t]
    for u in peers:
        tensor_copy(stat_out.at[u], stat_in, stat_send, stat_recv, u, u).wait_recv()
    mean_all = stat_in[0, 0:1, :]
    moment_all = stat_in[0, 1:2, :]
    weighted = stat_in[0, 2:3, :]
    for u in range(1, n_t):
        mean_all = mean_all + stat_in[u, 0:1, :]
        moment_all = moment_all + stat_in[u, 1:2, :]
        weighted = weighted + stat_in[u, 2:3, :]
    mean_all = mean_all / n_t
    for u in range(n_t):
        away = stat_in[u, 0:1, :] - mean_all
        moment_all = moment_all + cols * away * away
        total = total + to_col(away) * stat_in[u, 2:3, :]
    scale = to_col(lax.rsqrt(moment_all / depth + epsilon))
    mean_col = to_col(mean_all)
    for u in peers:
        tensor_copy(part_out.at[u], part_in, part_send, part_recv, u, u).wait_recv()
        total = total + part_in[u].astype(f32)
    product = scale * total
    preact = product + bias_ref[...]
    gate = 1.0 / (1.0 + jnp.exp(-preact))
    grad = (home[:, cols:].astype(f32) * gate * (1.0 + preact * (1.0 - gate))).astype(bf16)
    grads[t] = grad
    for u in peers:
        tensor_copy(grads.at[t], grads, grad_send, grad_recv, u, t).start()
    wide = grad.astype(f32)
    sums[t] = jnp.zeros(sums.shape[1:], f32)
    sums[t, 0:1, :] = to_row(jnp.sum(wide * weighted, axis=1, keepdims=True))
    sums[t, 1:2, :] = to_row(jnp.sum(wide * product, axis=1, keepdims=True))
    for u in peers:
        tensor_copy(sums.at[t], sums, sum_send, sum_recv, u, t).start()
    for u in peers:
        tensor_copy(sums.at[t], sums, sum_send, sum_recv, u, u).wait_recv()
    both = sums[0]
    for u in range(1, n_t):
        both = both + sums[u]
    mean_grad = to_col(both[0:1, :]) / depth
    mean_unit = to_col(both[1:2, :]) / depth * scale
    for u in peers:
        tensor_copy(grads.at[t], grads, grad_send, grad_recv, u, u).wait_recv()
    for c in range(0, cols, chunk):
        piece = rows_by_cols(grads[0], weights[0, c : c + chunk, :])
        for u in range(1, n_t):
            piece = piece + rows_by_cols(grads[u], weights[u, c : c + chunk, :])
        piece = piece * gain[:, c : c + chunk]
        away = home[:, c : c + chunk].astype(f32) - mean_col
        out_ref[:, c : c + chunk] = (scale * (piece - mean_grad - away * mean_unit)).astype(bf16)

    for u in peers:
        w_copy(u, t).wait_send()
        tensor_copy(stat_out.at[u], stat_in, stat_send, stat_recv, u, t).wait_send()
        tensor_copy(part_out.at[u], part_in, part_send, part_recv, u, t).wait_send()
        tensor_copy(grads.at[t], grads, grad_send, grad_recv, u, t).wait_send()
        tensor_copy(sums.at[t], sums, sum_send, sum_recv, u, t).wait_send()
    for j in dests:
        slot_copy(j, me).wait_send()
        row_copy(j, me).wait_send()


def per_device(inputs, upstream, proj_weight, proj_bias, norm_gain, home_rows):
    n_dp, n_t = lax.axis_size("dp"), lax.axis_size("tensor")
    rows, cols = inputs.shape
    head = upstream.shape[1]
    cap = max(2, 2 * rows // n_dp)
    width = cols + head
    line = max(rows, head)
    dma = pltpu.SemaphoreType.DMA
    in_vmem = pl.BlockSpec(memory_space=pltpu.VMEM)
    return pl.pallas_call(
        functools.partial(kernel, n_dp, n_t, cap),
        out_shape=jax.ShapeDtypeStruct((rows, cols), bf16),
        in_specs=[pl.BlockSpec(memory_space=pltpu.HBM)] * 6,
        out_specs=in_vmem,
        scratch_shapes=[
            pltpu.VMEM((rows, cols), bf16),
            pltpu.VMEM((rows, head), bf16),
            pltpu.VMEM((1, head), f32),
            pltpu.VMEM((1, cols), f32),
            pltpu.VMEM((1, rows), jnp.int32),
            pltpu.VMEM((n_t, cols, head), bf16),
            pltpu.VMEM((n_dp * cap, width), bf16),
            pltpu.VMEM((n_dp * cap, width), bf16),
            pltpu.VMEM((n_dp, 8, LANES), jnp.int32),
            pltpu.VMEM((n_dp, 8, LANES), jnp.int32),
            pltpu.VMEM((rows, width), bf16),
            pltpu.VMEM((rows, cols), bf16),
            pltpu.VMEM((n_t, rows, head), bf16),
            pltpu.VMEM((n_t, rows, head), bf16),
            pltpu.VMEM((n_t, 8, line), f32),
            pltpu.VMEM((n_t, 8, line), f32),
            pltpu.VMEM((n_t, rows, head), bf16),
            pltpu.VMEM((n_t, 8, line), f32),
        ]
        + [dma((n_t,))] * 2
        + [dma((n_dp,))] * 4
        + [dma((n_t,))] * 8
        + [dma((7,))],
        compiler_params=pltpu.CompilerParams(
            collective_id=0, has_side_effects=True, vmem_limit_bytes=64 * 1024 * 1024
        ),
        cost_estimate=pl.CostEstimate(
            flops=8 * rows * cols * head * n_t, bytes_accessed=2 * n_t * cols * head, transcendentals=rows * head
        ),
    )(
        inputs,
        upstream,
        proj_weight,
        proj_bias.reshape(1, head),
        norm_gain.reshape(1, n_t * cols),
        home_rows.reshape(1, rows),
    )


def solution(mesh):
    return jax.shard_map(
        per_device,
        mesh=mesh,
        in_specs=(
            P("dp", "tensor"),
            P("dp", "tensor"),
            P(None, "tensor"),
            P("tensor"),
            P(),
            P("dp"),
        ),
        out_specs=P("dp", "tensor"),
        check_vma=False,
    )
```

```python
import functools
import math

import jax
import jax.numpy as jnp
from jax import lax
from jax.experimental import pallas as pl
from jax.experimental.pallas import tpu as pltpu
from jax.sharding import PartitionSpec as P

epsilon = 1e-05
MESH = pl.DeviceIdType.MESH
f32, bf16 = jnp.float32, jnp.bfloat16
LANES = 128


def rows_by_cols(left, right):
    return lax.dot_general(
        left, right, (((1,), (1,)), ((), ())), preferred_element_type=f32
    )


def kernel(
    n_dp, n_t, cap,
    x_hbm, up_hbm, w_ref, bias_hbm, gain_hbm, hr_hbm,
    out_ref,
    blocks, up_ref, bias_ref, gain_ref, hr_ref, w_head,
    weights, packed, arrived, slots_out, slots_in, facts_out, facts_in,
    centred, grads_out, grads_in, grads, sums,
    x_send, x_recv, x_pass, w_send, w_recv, w_pass, w_got, near_send, near_recv,
    row_send, row_recv, slot_send, slot_recv, fact_send, fact_recv, back_send, back_recv,
    grad_send, grad_recv, sum_send, sum_recv,
    local_sem,
):
    me = lax.axis_index("dp")
    t = lax.axis_index("tensor")
    rows, head = up_ref.shape
    cols = blocks.shape[2]
    depth = n_t * cols
    per = LANES // cap
    chunk = math.gcd(cols, 256)
    first = 2 * cols // 3 // LANES * LANES
    parts = [(0, first), (first, cols - first)]
    quarter = cols // 4

    def sibling(u):
        return u + 1 - 2 * lax.rem(u, 2)

    across_peers = [lax.rem(t + 2 * k, n_t) for k in range(1, n_t // 2)]
    other_peers = [sibling(u) for u in across_peers]
    far = [u for pair in zip(across_peers, other_peers) for u in pair]
    near = sibling(t)
    peers = far + [near]
    partner = sibling(me)
    half = lax.rem(me, 2)
    dests = [lax.rem(me + d, n_dp) for d in range(1, n_dp)]
    sources = [lax.rem(me + n_dp - d, n_dp) for d in range(1, n_dp)]

    barrier = pltpu.get_barrier_semaphore()
    for u in peers:
        pl.semaphore_signal(barrier, inc=1, device_id={"tensor": u}, device_id_type=MESH)
    for j in dests:
        pl.semaphore_signal(barrier, inc=1, device_id={"dp": j}, device_id_type=MESH)

    fetches = [
        pltpu.make_async_copy(src, dst, local_sem.at[k])
        for k, (src, dst) in enumerate(
            [
                (hr_hbm, hr_ref),
                (x_hbm, blocks.at[t]),
                (up_hbm, up_ref),
                (gain_hbm, gain_ref),
                (bias_hbm, bias_ref),
                (w_ref, w_head),
                (w_ref.at[pl.ds(pl.multiple_of(t * cols, LANES), cols)], weights.at[t]),
            ]
        )
    ]
    for fetch in fetches:
        fetch.start()

    fetches[0].wait()
    hr_row = hr_ref[...]
    down = lax.broadcasted_iota(jnp.int32, (rows, rows), 0)
    across = lax.broadcasted_iota(jnp.int32, (rows, rows), 1)
    eye = down == across

    def to_row(column):
        return jnp.sum(jnp.where(eye, column, 0.0), axis=0, keepdims=True)

    def to_col(line):
        return jnp.sum(jnp.where(eye, line, 0.0), axis=1, keepdims=True)

    hr_col = to_col(hr_row.astype(f32)).astype(jnp.int32)
    owner_col, owner_row = hr_col // rows, hr_row // rows
    slot_col = hr_col - owner_col * rows
    same = owner_col == owner_row
    rank_row = jnp.sum(jnp.where(same & (down < across), 1.0, 0.0), axis=0, keepdims=True).astype(jnp.int32)
    rank_col = jnp.sum(jnp.where(same & (across < down), 1.0, 0.0), axis=1, keepdims=True).astype(jnp.int32)
    target_row = owner_row * cap + rank_row
    total_slots = n_dp * cap
    placing = jnp.where(
        lax.broadcasted_iota(jnp.int32, (total_slots, rows), 0) == target_row, 1.0, 0.0
    ).astype(bf16)
    fetches[1].wait()
    for c in range(0, cols, chunk):
        packed[:, c : c + chunk] = jnp.dot(
            placing, blocks[t, :, c : c + chunk], preferred_element_type=f32
        ).astype(bf16)
    lane = lax.broadcasted_iota(jnp.int32, (rows, LANES), 1)
    my_lane = lax.rem(me, per) * cap

    def in_lanes(j, column):
        hit = (owner_col == j) & (rank_col + my_lane == lane)
        return jnp.sum(jnp.where(hit, column, 0.0), axis=0, keepdims=True)

    for j in range(n_dp):
        slots_out[j] = jnp.broadcast_to(in_lanes(j, slot_col.astype(f32) + 1.0), (8, LANES)).astype(jnp.int32)

    def remote(src, dst, send, recv, to):
        return pltpu.make_async_remote_copy(
            src_ref=src, dst_ref=dst, send_sem=send, recv_sem=recv, device_id=to, device_id_type=MESH
        )

    def x_copy(u, block):
        return remote(blocks.at[block], blocks.at[block], x_send.at[u], x_recv.at[block], {"tensor": u})

    def x_forward(block):
        return remote(blocks.at[block], blocks.at[block], x_pass.at[block], x_recv.at[block], {"tensor": near})

    def near_copy(block):
        return remote(
            w_ref.at[pl.ds(pl.multiple_of(near * cols, LANES), cols)], weights.at[block],
            near_send.at[0], near_recv.at[0], {"tensor": near},
        )

    def w_span(which, q):
        return pl.ds(pl.multiple_of((2 * which + q) * quarter, 16), quarter)

    def w_copy(u, block, q):
        start = pl.multiple_of(u * cols + (2 * half + q) * quarter, 16)
        return remote(
            w_ref.at[pl.ds(start, quarter)], weights.at[block, w_span(half, q)],
            w_send.at[u, q], w_recv.at[block, q], {"tensor": u},
        )

    def w_forward(block, q, which):
        return remote(
            weights.at[block, w_span(which, q)], weights.at[block, w_span(which, q)],
            w_pass.at[block, q], w_got.at[block, q], {"dp": partner},
        )

    def row_copy(j, source, k):
        begin, size = parts[k]
        return remote(
            packed.at[pl.ds(pl.multiple_of(j * cap, 16), cap), pl.ds(begin, size)],
            arrived.at[pl.ds(pl.multiple_of(source * cap, 16), cap), pl.ds(begin, size)],
            row_send.at[k, j], row_recv.at[k, source], {"dp": j},
        )

    def back_copy(j, source):
        return remote(
            grads_out.at[pl.ds(pl.multiple_of(j * cap, 16), cap)],
            grads_in.at[pl.ds(pl.multiple_of(source * cap, 16), cap)],
            back_send.at[j], back_recv.at[source], {"dp": j},
        )

    def slot_copy(j, source):
        return remote(slots_out.at[j], slots_in.at[source], slot_send.at[j], slot_recv.at[source], {"dp": j})

    def fact_copy(j, source):
        return remote(facts_out.at[j], facts_in.at[source], fact_send.at[j], fact_recv.at[source], {"dp": j})

    def grad_copy(u, block):
        return remote(grads.at[block], grads.at[block], grad_send.at[u], grad_recv.at[block], {"tensor": u})

    def sum_copy(u, block):
        return remote(sums.at[block], sums.at[block], sum_send.at[u], sum_recv.at[block], {"tensor": u})

    pl.semaphore_wait(barrier, len(peers) + len(dests))
    for u in across_peers:
        x_copy(u, t).start()
    x_copy(near, t).start()
    for j in dests:
        slot_copy(j, me).start()
        row_copy(j, me, 0).start()
    near_copy(t).start()
    own_rows = pltpu.make_async_copy(
        packed.at[pl.ds(pl.multiple_of(me * cap, 16), cap)],
        arrived.at[pl.ds(pl.multiple_of(me * cap, 16), cap)],
        local_sem.at[7],
    )
    own_rows.start()
    slots_in[me] = slots_out[me]

    for fetch in fetches[2:]:
        fetch.wait()
    weighted = jnp.zeros((1, head), f32)
    which = lax.broadcasted_iota(jnp.int32, (16, cols), 0)
    for b in range(n_t):
        gain = gain_ref[:, b * cols : (b + 1) * cols]
        gain_hi = gain.astype(bf16).astype(f32)
        gain_mid = (gain - gain_hi).astype(bf16).astype(f32)
        gain_lo = gain - gain_hi - gain_mid
        gain_parts = jnp.where(
            which == 0, gain_hi, jnp.where(which == 1, gain_mid, jnp.where(which == 2, gain_lo, 0.0))
        ).astype(bf16)
        line = jnp.dot(gain_parts, w_head[b * cols : (b + 1) * cols, :], preferred_element_type=f32)
        weighted = weighted + jnp.sum(line, axis=0, keepdims=True)

    for u in across_peers:
        x_copy(u, u).wait_recv()
        x_forward(u).start()
    for q in range(2):
        for u in far:
            w_copy(u, t, q).start()
    x_copy(near, near).wait_recv()
    for u in other_peers:
        x_forward(u).wait_recv()
    running = jnp.zeros((rows, LANES), f32)
    for b in range(n_t):
        for c in range(0, cols, LANES):
            running = running + blocks[b, :, c : c + LANES].astype(f32)
    mean_here = jnp.sum(running, axis=1, keepdims=True) / depth
    running = jnp.zeros((rows, LANES), f32)
    total = jnp.zeros((rows, head), f32)
    for b in range(n_t):
        for c in range(0, cols, LANES):
            piece = blocks[b, :, c : c + LANES].astype(f32) - mean_here
            gain = gain_ref[:, b * cols + c : b * cols + c + LANES]
            centred[:, c : c + LANES] = (piece * gain).astype(bf16)
            running = running + piece * piece
        total = total + jnp.dot(
            centred[...], w_head[b * cols : (b + 1) * cols, :], preferred_element_type=f32
        )
    scale_here = lax.rsqrt(jnp.sum(running, axis=1, keepdims=True) / depth + epsilon)
    product = scale_here * total
    preact = product + bias_ref[...]
    gate = 1.0 / (1.0 + jnp.exp(-preact))
    grad = (up_ref[...].astype(f32) * gate * (1.0 + preact * (1.0 - gate))).astype(bf16)
    grads_out[...] = jnp.dot(placing, grad, preferred_element_type=f32).astype(bf16)
    wide = grad.astype(f32)
    facts = [
        mean_here,
        scale_here,
        jnp.sum(wide * weighted, axis=1, keepdims=True),
        jnp.sum(wide * product, axis=1, keepdims=True),
    ]
    for j in range(n_dp):
        facts_out[j] = jnp.zeros((8, LANES), f32)
        for k, fact in enumerate(facts):
            facts_out[j, k : k + 1, :] = in_lanes(j, fact)
    for j in dests:
        back_copy(j, me).start()
        fact_copy(j, me).start()
    for j in dests:
        row_copy(j, me, 1).start()
    own_grads = pltpu.make_async_copy(
        grads_out.at[pl.ds(pl.multiple_of(me * cap, 16), cap)],
        grads_in.at[pl.ds(pl.multiple_of(me * cap, 16), cap)],
        local_sem.at[8],
    )
    own_grads.start()
    facts_in[me] = facts_out[me]
    for u in far:
        w_copy(u, u, 0).wait_recv()
        w_forward(u, 0, half).start()

    def lines_of(ref, row):
        lines = []
        for g in range(n_dp // per):
            line = ref[g * per, row : row + 1, :]
            for k in range(1, per):
                line = line + ref[g * per + k, row : row + 1, :]
            lines.append(line)
        return jnp.concatenate(lines, axis=1)

    for i in sources:
        slot_copy(i, i).wait_recv()
    landed = lax.broadcasted_iota(jnp.int32, (rows, total_slots), 0) == lines_of(slots_in, 0) - 1
    landing = jnp.where(landed, 1.0, 0.0).astype(bf16)

    def at_home(row):
        return jnp.sum(jnp.where(landed, lines_of(facts_in, row), 0.0), axis=1, keepdims=True)

    own_grads.wait()
    for i in sources:
        back_copy(i, i).wait_recv()
    grads[t] = jnp.dot(landing, grads_in[...], preferred_element_type=f32).astype(bf16)
    for u in peers:
        grad_copy(u, t).start()
    for i in sources:
        fact_copy(i, i).wait_recv()
    sums[t] = jnp.zeros(sums.shape[1:], f32)
    sums[t, 0:1, :] = to_row(at_home(2))
    sums[t, 1:2, :] = to_row(at_home(3))
    for u in peers:
        sum_copy(u, t).start()
    mean_col, scale = at_home(0), at_home(1)
    for u in far:
        w_copy(u, u, 1).wait_recv()
        w_forward(u, 1, half).start()
    for u in peers:
        sum_copy(u, u).wait_recv()
    both = sums[0]
    for u in range(1, n_t):
        both = both + sums[u]
    mean_grad = to_col(both[0:1, :]) / depth
    mean_unit = to_col(both[1:2, :]) / depth * scale
    for u in peers:
        grad_copy(u, u).wait_recv()
    near_copy(near).wait_recv()
    for q in range(2):
        for u in far:
            w_forward(u, q, 1 - half).wait_recv()
    own_rows.wait()
    for k in range(2):
        for i in sources:
            row_copy(i, i, k).wait_recv()
    for c in range(0, cols, chunk):
        piece = rows_by_cols(grads[0], weights[0, c : c + chunk, :])
        for u in range(1, n_t):
            piece = piece + rows_by_cols(grads[u], weights[u, c : c + chunk, :])
        piece = piece * gain_ref[:, pl.ds(pl.multiple_of(t * cols + c, LANES), chunk)]
        away = jnp.dot(landing, arrived[:, c : c + chunk], preferred_element_type=f32) - mean_col
        out_ref[:, c : c + chunk] = (scale * (piece - mean_grad - away * mean_unit)).astype(bf16)

    for u in across_peers + [near]:
        x_copy(u, t).wait_send()
    for u in across_peers:
        x_forward(u).wait_send()
    near_copy(t).wait_send()
    for u in far:
        for q in range(2):
            w_copy(u, t, q).wait_send()
            w_forward(u, q, half).wait_send()
    for u in peers:
        grad_copy(u, t).wait_send()
        sum_copy(u, t).wait_send()
    for j in dests:
        slot_copy(j, me).wait_send()
        fact_copy(j, me).wait_send()
        back_copy(j, me).wait_send()
        for k in range(2):
            row_copy(j, me, k).wait_send()


def per_device(inputs, upstream, proj_weight, proj_bias, norm_gain, home_rows):
    n_dp, n_t = lax.axis_size("dp"), lax.axis_size("tensor")
    rows, cols = inputs.shape
    head = upstream.shape[1]
    cap = max(2, 2 * rows // n_dp)
    dma = pltpu.SemaphoreType.DMA
    in_vmem = pl.BlockSpec(memory_space=pltpu.VMEM)
    return pl.pallas_call(
        functools.partial(kernel, n_dp, n_t, cap),
        out_shape=jax.ShapeDtypeStruct((rows, cols), bf16),
        in_specs=[pl.BlockSpec(memory_space=pltpu.HBM)] * 6,
        out_specs=in_vmem,
        scratch_shapes=[
            pltpu.VMEM((n_t, rows, cols), bf16),
            pltpu.VMEM((rows, head), bf16),
            pltpu.VMEM((1, head), f32),
            pltpu.VMEM((1, n_t * cols), f32),
            pltpu.VMEM((1, rows), jnp.int32),
            pltpu.VMEM((n_t * cols, head), bf16),
            pltpu.VMEM((n_t, cols, head), bf16),
            pltpu.VMEM((n_dp * cap, cols), bf16),
            pltpu.VMEM((n_dp * cap, cols), bf16),
            pltpu.VMEM((n_dp, 8, LANES), jnp.int32),
            pltpu.VMEM((n_dp, 8, LANES), jnp.int32),
            pltpu.VMEM((n_dp, 8, LANES), f32),
            pltpu.VMEM((n_dp, 8, LANES), f32),
            pltpu.VMEM((rows, cols), bf16),
            pltpu.VMEM((n_dp * cap, head), bf16),
            pltpu.VMEM((n_dp * cap, head), bf16),
            pltpu.VMEM((n_t, rows, head), bf16),
            pltpu.VMEM((n_t, 8, rows), f32),
        ]
        + [dma((n_t,))] * 3
        + [dma((n_t, 2))] * 4
        + [dma((1,))] * 2
        + [dma((2, n_dp))] * 2
        + [dma((n_dp,))] * 6
        + [dma((n_t,))] * 4
        + [dma((9,))],
        compiler_params=pltpu.CompilerParams(
            collective_id=0, has_side_effects=True, vmem_limit_bytes=64 * 1024 * 1024
        ),
        cost_estimate=pl.CostEstimate(
            flops=8 * rows * cols * head * n_t, bytes_accessed=2 * n_t * cols * head, transcendentals=rows * head
        ),
    )(
        inputs,
        upstream,
        proj_weight,
        proj_bias.reshape(1, head),
        norm_gain.reshape(1, n_t * cols),
        home_rows.reshape(1, rows),
    )


def solution(mesh):
    return jax.shard_map(
        per_device,
        mesh=mesh,
        in_specs=(
            P("dp", "tensor"),
            P("dp", "tensor"),
            P(None, "tensor"),
            P("tensor"),
            P(),
            P("dp"),
        ),
        out_specs=P("dp", "tensor"),
        check_vma=False,
    )
```

```python
import functools
import math

import jax
import jax.numpy as jnp
from jax import lax
from jax.experimental import pallas as pl
from jax.experimental.pallas import tpu as pltpu
from jax.sharding import PartitionSpec as P

epsilon = 1e-05
MESH = pl.DeviceIdType.MESH
f32, bf16 = jnp.float32, jnp.bfloat16
LANES = 128


def rows_by_cols(left, right):
    return lax.dot_general(
        left, right, (((1,), (1,)), ((), ())), preferred_element_type=f32
    )


def kernel(
    n_dp, n_t, cap,
    x_hbm, up_hbm, w_ref, bias_hbm, gain_hbm, hr_hbm,
    out_ref,
    blocks, up_ref, bias_ref, gain_ref, hr_ref, w_head,
    weights, packed, arrived, slots_out, slots_in, facts_out, facts_in,
    centred, grads_out, grads_in, grads, sums,
    x_send, x_recv, x_pass, w_send, w_recv, w_pass, w_got, near_send, near_recv,
    row_send, row_recv, slot_send, slot_recv, fact_send, fact_recv, back_send, back_recv,
    grad_send, grad_recv, sum_send, sum_recv,
    local_sem,
):
    me = lax.axis_index("dp")
    t = lax.axis_index("tensor")
    rows, head = up_ref.shape
    cols = blocks.shape[2]
    depth = n_t * cols
    per = LANES // cap
    chunk = math.gcd(cols, 256)
    first = 2 * cols // 3 // LANES * LANES
    parts = [(0, first), (first, cols - first)]
    pieces = 4
    quarter = cols // (2 * pieces)

    def sibling(u):
        return u + 1 - 2 * lax.rem(u, 2)

    across_peers = [lax.rem(t + 2 * k, n_t) for k in range(1, n_t // 2)]
    other_peers = [sibling(u) for u in across_peers]
    far = [u for pair in zip(across_peers, other_peers) for u in pair]
    near = sibling(t)
    peers = far + [near]
    partner = sibling(me)
    half = lax.rem(me, 2)
    dests = [lax.rem(me + d, n_dp) for d in range(1, n_dp)]
    sources = [lax.rem(me + n_dp - d, n_dp) for d in range(1, n_dp)]

    barrier = pltpu.get_barrier_semaphore()
    for u in peers:
        pl.semaphore_signal(barrier, inc=1, device_id={"tensor": u}, device_id_type=MESH)
    for j in dests:
        pl.semaphore_signal(barrier, inc=1, device_id={"dp": j}, device_id_type=MESH)

    fetches = [
        pltpu.make_async_copy(src, dst, local_sem.at[k])
        for k, (src, dst) in enumerate(
            [
                (hr_hbm, hr_ref),
                (x_hbm, blocks.at[t]),
                (up_hbm, up_ref),
                (gain_hbm, gain_ref),
                (bias_hbm, bias_ref),
                (w_ref, w_head),
                (w_ref.at[pl.ds(pl.multiple_of(t * cols, LANES), cols)], weights.at[t]),
            ]
        )
    ]
    for fetch in fetches:
        fetch.start()

    fetches[0].wait()
    hr_row = hr_ref[...]
    down = lax.broadcasted_iota(jnp.int32, (rows, rows), 0)
    across = lax.broadcasted_iota(jnp.int32, (rows, rows), 1)
    eye = down == across

    def to_row(column):
        return jnp.sum(jnp.where(eye, column, 0.0), axis=0, keepdims=True)

    def to_col(line):
        return jnp.sum(jnp.where(eye, line, 0.0), axis=1, keepdims=True)

    hr_col = to_col(hr_row.astype(f32)).astype(jnp.int32)
    owner_col, owner_row = hr_col // rows, hr_row // rows
    slot_col = hr_col - owner_col * rows
    same = owner_col == owner_row
    rank_row = jnp.sum(jnp.where(same & (down < across), 1.0, 0.0), axis=0, keepdims=True).astype(jnp.int32)
    rank_col = jnp.sum(jnp.where(same & (across < down), 1.0, 0.0), axis=1, keepdims=True).astype(jnp.int32)
    target_row = owner_row * cap + rank_row
    total_slots = n_dp * cap
    placing = jnp.where(
        lax.broadcasted_iota(jnp.int32, (total_slots, rows), 0) == target_row, 1.0, 0.0
    ).astype(bf16)
    fetches[1].wait()
    for c in range(0, cols, chunk):
        packed[:, c : c + chunk] = jnp.dot(
            placing, blocks[t, :, c : c + chunk], preferred_element_type=f32
        ).astype(bf16)
    lane = lax.broadcasted_iota(jnp.int32, (rows, LANES), 1)
    my_lane = lax.rem(me, per) * cap

    def in_lanes(j, column):
        hit = (owner_col == j) & (rank_col + my_lane == lane)
        return jnp.sum(jnp.where(hit, column, 0.0), axis=0, keepdims=True)

    for j in range(n_dp):
        slots_out[j] = jnp.broadcast_to(in_lanes(j, slot_col.astype(f32) + 1.0), (8, LANES)).astype(jnp.int32)

    def remote(src, dst, send, recv, to):
        return pltpu.make_async_remote_copy(
            src_ref=src, dst_ref=dst, send_sem=send, recv_sem=recv, device_id=to, device_id_type=MESH
        )

    def x_copy(u, block):
        return remote(blocks.at[block], blocks.at[block], x_send.at[u], x_recv.at[block], {"tensor": u})

    def x_forward(block):
        return remote(blocks.at[block], blocks.at[block], x_pass.at[block], x_recv.at[block], {"tensor": near})

    def near_copy(block):
        return remote(
            w_ref.at[pl.ds(pl.multiple_of(near * cols, LANES), cols)], weights.at[block],
            near_send.at[0], near_recv.at[0], {"tensor": near},
        )

    def w_span(which, q):
        return pl.ds(pl.multiple_of((pieces * which + q) * quarter, 16), quarter)

    def w_copy(u, block, q):
        start = pl.multiple_of(u * cols + (pieces * half + q) * quarter, 16)
        return remote(
            w_ref.at[pl.ds(start, quarter)], weights.at[block, w_span(half, q)],
            w_send.at[u, q], w_recv.at[block, q], {"tensor": u},
        )

    def w_forward(block, q, which):
        return remote(
            weights.at[block, w_span(which, q)], weights.at[block, w_span(which, q)],
            w_pass.at[block, q], w_got.at[block, q], {"dp": partner},
        )

    def row_copy(j, source, k):
        begin, size = parts[k]
        return remote(
            packed.at[pl.ds(pl.multiple_of(j * cap, 16), cap), pl.ds(begin, size)],
            arrived.at[pl.ds(pl.multiple_of(source * cap, 16), cap), pl.ds(begin, size)],
            row_send.at[k, j], row_recv.at[k, source], {"dp": j},
        )

    def back_copy(j, source):
        return remote(
            grads_out.at[pl.ds(pl.multiple_of(j * cap, 16), cap)],
            grads_in.at[pl.ds(pl.multiple_of(source * cap, 16), cap)],
            back_send.at[j], back_recv.at[source], {"dp": j},
        )

    def slot_copy(j, source):
        return remote(slots_out.at[j], slots_in.at[source], slot_send.at[j], slot_recv.at[source], {"dp": j})

    def fact_copy(j, source):
        return remote(facts_out.at[j], facts_in.at[source], fact_send.at[j], fact_recv.at[source], {"dp": j})

    def grad_copy(u, block):
        return remote(grads.at[block], grads.at[block], grad_send.at[u], grad_recv.at[block], {"tensor": u})

    def sum_copy(u, block):
        return remote(sums.at[block], sums.at[block], sum_send.at[u], sum_recv.at[block], {"tensor": u})

    pl.semaphore_wait(barrier, len(peers) + len(dests))
    for u in across_peers:
        x_copy(u, t).start()
    x_copy(near, t).start()
    for j in dests:
        slot_copy(j, me).start()
        row_copy(j, me, 0).start()
    for j in dests:
        row_copy(j, me, 1).start()
    near_copy(t).start()
    own_rows = pltpu.make_async_copy(
        packed.at[pl.ds(pl.multiple_of(me * cap, 16), cap)],
        arrived.at[pl.ds(pl.multiple_of(me * cap, 16), cap)],
        local_sem.at[7],
    )
    own_rows.start()
    slots_in[me] = slots_out[me]

    for fetch in fetches[2:]:
        fetch.wait()
    weighted = jnp.zeros((1, head), f32)
    which = lax.broadcasted_iota(jnp.int32, (16, cols), 0)
    for b in range(n_t):
        gain = gain_ref[:, b * cols : (b + 1) * cols]
        gain_hi = gain.astype(bf16).astype(f32)
        gain_mid = (gain - gain_hi).astype(bf16).astype(f32)
        gain_lo = gain - gain_hi - gain_mid
        gain_parts = jnp.where(
            which == 0, gain_hi, jnp.where(which == 1, gain_mid, jnp.where(which == 2, gain_lo, 0.0))
        ).astype(bf16)
        line = jnp.dot(gain_parts, w_head[b * cols : (b + 1) * cols, :], preferred_element_type=f32)
        weighted = weighted + jnp.sum(line, axis=0, keepdims=True)

    for u in across_peers:
        x_copy(u, u).wait_recv()
        x_forward(u).start()
    for q in range(pieces):
        for u in far:
            w_copy(u, t, q).start()
    x_copy(near, near).wait_recv()
    for u in other_peers:
        x_forward(u).wait_recv()
    running = jnp.zeros((rows, LANES), f32)
    for b in range(n_t):
        for c in range(0, cols, LANES):
            running = running + blocks[b, :, c : c + LANES].astype(f32)
    mean_here = jnp.sum(running, axis=1, keepdims=True) / depth
    running = jnp.zeros((rows, LANES), f32)
    total = jnp.zeros((rows, head), f32)
    for b in range(n_t):
        for c in range(0, cols, LANES):
            piece = blocks[b, :, c : c + LANES].astype(f32) - mean_here
            gain = gain_ref[:, b * cols + c : b * cols + c + LANES]
            centred[:, c : c + LANES] = (piece * gain).astype(bf16)
            running = running + piece * piece
        total = total + jnp.dot(
            centred[...], w_head[b * cols : (b + 1) * cols, :], preferred_element_type=f32
        )
    scale_here = lax.rsqrt(jnp.sum(running, axis=1, keepdims=True) / depth + epsilon)
    product = scale_here * total
    preact = product + bias_ref[...]
    gate = 1.0 / (1.0 + jnp.exp(-preact))
    grad = (up_ref[...].astype(f32) * gate * (1.0 + preact * (1.0 - gate))).astype(bf16)
    grads_out[...] = jnp.dot(placing, grad, preferred_element_type=f32).astype(bf16)
    wide = grad.astype(f32)
    facts = [
        mean_here,
        scale_here,
        jnp.sum(wide * weighted, axis=1, keepdims=True),
        jnp.sum(wide * product, axis=1, keepdims=True),
    ]
    for j in range(n_dp):
        facts_out[j] = jnp.zeros((8, LANES), f32)
        for k, fact in enumerate(facts):
            facts_out[j, k : k + 1, :] = in_lanes(j, fact)
    for j in dests:
        back_copy(j, me).start()
        fact_copy(j, me).start()
    own_grads = pltpu.make_async_copy(
        grads_out.at[pl.ds(pl.multiple_of(me * cap, 16), cap)],
        grads_in.at[pl.ds(pl.multiple_of(me * cap, 16), cap)],
        local_sem.at[8],
    )
    own_grads.start()
    facts_in[me] = facts_out[me]
    def pass_on(q):
        for u in far:
            w_copy(u, u, q).wait_recv()
            w_forward(u, q, half).start()

    pass_on(0)
    pass_on(1)

    def lines_of(ref, row):
        lines = []
        for g in range(n_dp // per):
            line = ref[g * per, row : row + 1, :]
            for k in range(1, per):
                line = line + ref[g * per + k, row : row + 1, :]
            lines.append(line)
        return jnp.concatenate(lines, axis=1)

    for i in sources:
        slot_copy(i, i).wait_recv()
    landed = lax.broadcasted_iota(jnp.int32, (rows, total_slots), 0) == lines_of(slots_in, 0) - 1
    landing = jnp.where(landed, 1.0, 0.0).astype(bf16)

    def at_home(row):
        return jnp.sum(jnp.where(landed, lines_of(facts_in, row), 0.0), axis=1, keepdims=True)

    pass_on(2)
    own_grads.wait()
    for i in sources:
        back_copy(i, i).wait_recv()
    grads[t] = jnp.dot(landing, grads_in[...], preferred_element_type=f32).astype(bf16)
    for u in peers:
        grad_copy(u, t).start()
    for i in sources:
        fact_copy(i, i).wait_recv()
    sums[t] = jnp.zeros(sums.shape[1:], f32)
    sums[t, 0:1, :] = to_row(at_home(2))
    sums[t, 1:2, :] = to_row(at_home(3))
    for u in peers:
        sum_copy(u, t).start()
    mean_col, scale = at_home(0), at_home(1)
    pass_on(3)
    for u in peers:
        sum_copy(u, u).wait_recv()
    both = sums[0]
    for u in range(1, n_t):
        both = both + sums[u]
    mean_grad = to_col(both[0:1, :]) / depth
    mean_unit = to_col(both[1:2, :]) / depth * scale
    for u in peers:
        grad_copy(u, u).wait_recv()
    near_copy(near).wait_recv()
    own_rows.wait()
    for k in range(2):
        for i in sources:
            row_copy(i, i, k).wait_recv()
    for c in range(0, cols, chunk):
        centred[:, c : c + chunk] = jnp.dot(
            landing, arrived[:, c : c + chunk], preferred_element_type=f32
        ).astype(bf16)
    for q in range(pieces):
        for u in far:
            w_forward(u, q, 1 - half).wait_recv()
    for c in range(0, cols, chunk):
        piece = rows_by_cols(grads[0], weights[0, c : c + chunk, :])
        for u in range(1, n_t):
            piece = piece + rows_by_cols(grads[u], weights[u, c : c + chunk, :])
        piece = piece * gain_ref[:, pl.ds(pl.multiple_of(t * cols + c, LANES), chunk)]
        away = centred[:, c : c + chunk].astype(f32) - mean_col
        out_ref[:, c : c + chunk] = (scale * (piece - mean_grad - away * mean_unit)).astype(bf16)

    for u in across_peers + [near]:
        x_copy(u, t).wait_send()
    for u in across_peers:
        x_forward(u).wait_send()
    near_copy(t).wait_send()
    for u in far:
        for q in range(pieces):
            w_copy(u, t, q).wait_send()
            w_forward(u, q, half).wait_send()
    for u in peers:
        grad_copy(u, t).wait_send()
        sum_copy(u, t).wait_send()
    for j in dests:
        slot_copy(j, me).wait_send()
        fact_copy(j, me).wait_send()
        back_copy(j, me).wait_send()
        for k in range(2):
            row_copy(j, me, k).wait_send()


def per_device(inputs, upstream, proj_weight, proj_bias, norm_gain, home_rows):
    n_dp, n_t = lax.axis_size("dp"), lax.axis_size("tensor")
    rows, cols = inputs.shape
    head = upstream.shape[1]
    cap = max(2, 2 * rows // n_dp)
    dma = pltpu.SemaphoreType.DMA
    in_vmem = pl.BlockSpec(memory_space=pltpu.VMEM)
    return pl.pallas_call(
        functools.partial(kernel, n_dp, n_t, cap),
        out_shape=jax.ShapeDtypeStruct((rows, cols), bf16),
        in_specs=[pl.BlockSpec(memory_space=pltpu.HBM)] * 6,
        out_specs=in_vmem,
        scratch_shapes=[
            pltpu.VMEM((n_t, rows, cols), bf16),
            pltpu.VMEM((rows, head), bf16),
            pltpu.VMEM((1, head), f32),
            pltpu.VMEM((1, n_t * cols), f32),
            pltpu.VMEM((1, rows), jnp.int32),
            pltpu.VMEM((n_t * cols, head), bf16),
            pltpu.VMEM((n_t, cols, head), bf16),
            pltpu.VMEM((n_dp * cap, cols), bf16),
            pltpu.VMEM((n_dp * cap, cols), bf16),
            pltpu.VMEM((n_dp, 8, LANES), jnp.int32),
            pltpu.VMEM((n_dp, 8, LANES), jnp.int32),
            pltpu.VMEM((n_dp, 8, LANES), f32),
            pltpu.VMEM((n_dp, 8, LANES), f32),
            pltpu.VMEM((rows, cols), bf16),
            pltpu.VMEM((n_dp * cap, head), bf16),
            pltpu.VMEM((n_dp * cap, head), bf16),
            pltpu.VMEM((n_t, rows, head), bf16),
            pltpu.VMEM((n_t, 8, rows), f32),
        ]
        + [dma((n_t,))] * 3
        + [dma((n_t, 4))] * 4
        + [dma((1,))] * 2
        + [dma((2, n_dp))] * 2
        + [dma((n_dp,))] * 6
        + [dma((n_t,))] * 4
        + [dma((9,))],
        compiler_params=pltpu.CompilerParams(
            collective_id=0, has_side_effects=True, vmem_limit_bytes=63 * 1024 * 1024
        ),
        cost_estimate=pl.CostEstimate(
            flops=8 * rows * cols * head * n_t, bytes_accessed=2 * n_t * cols * head, transcendentals=rows * head
        ),
    )(
        inputs,
        upstream,
        proj_weight,
        proj_bias.reshape(1, head),
        norm_gain.reshape(1, n_t * cols),
        home_rows.reshape(1, rows),
    )


def solution(mesh):
    return jax.shard_map(
        per_device,
        mesh=mesh,
        in_specs=(
            P("dp", "tensor"),
            P("dp", "tensor"),
            P(None, "tensor"),
            P("tensor"),
            P(),
            P("dp"),
        ),
        out_specs=P("dp", "tensor"),
        check_vma=False,
    )
```
